256 devices in a mesh: layer: 32 (over z, x), iface: 8 (over y, core).
Axes of the slice: x: 4, y: 4, z: 8, core: 2. Of those that a mesh axis runs over, the one named last changes fastest.
Arguments:
- green_down: bfloat16 [32, 2, 2048, 2048], P('layer', None, 'iface'), may hold values from -0.09375 to 0.09375
- green_up: bfloat16 [32, 2, 2048, 2048], P('layer', None, 'iface'), may hold values from -0.09375 to 0.09375
- source_down: bfloat16 [32, 2, 96, 2048], P('layer', None, None, 'iface'), may hold values from -2 to 2
- source_up: bfloat16 [32, 2, 96, 2048], P('layer', None, None, 'iface'), may hold values from -2 to 2
Outputs:
- down_traces: bfloat16 [32, 2, 96, 2048], P('layer', None, None, 'iface')
- up_traces: bfloat16 [32, 2, 96, 2048], P('layer', None, None, 'iface')
The draws below stay inside these ranges and needn't reach their ends.
All inputs are finite; a program needn't handle non-finite values.
Results may differ from the reference program's by a relative error of at most 0.027.
Values may be sent and summed in bfloat16 or wider, within the bound.
A program may use at most 64 MiB of HBM per device.

```python
import jax
import jax.numpy as jnp
from jax import lax

SHOTS = 96
NPTS = 2048
LAYERS = 32


def level_of(rng, extent, shards, least, largest):
    loudness = 1.0
    for axis_at, shards_of in shards:
        steps = jax.random.uniform(jax.random.fold_in(jax.random.fold_in(rng, 6), axis_at), (shards_of,), jnp.float32, least / len(shards), largest / len(shards))
        loudness = loudness * jnp.repeat(jnp.exp(steps), extent[axis_at] // shards_of).reshape((-1,) + (1,) * (len(extent) - 1 - axis_at))
    return loudness


def bell_draw(own_key, extent, deviation, limit, shards=(), dtype=jnp.bfloat16):
    level = level_of(own_key, extent, shards, -0.22, 0.18) if shards else 1.0
    drawn = jax.random.normal(own_key, extent, jnp.float32) * deviation * level
    return jnp.minimum(jnp.maximum(drawn, -limit), limit).astype(dtype)


def setup_inputs(seed: int = 0) -> dict:
    splits = jax.random.split(jax.random.key(seed), 5)
    return {
        "green_down": bell_draw(splits[0], (LAYERS, 2, NPTS, NPTS), (2 * NPTS + NPTS // 8) ** -0.5, 0.09375, ((0, 32), (2, 8))),
        "green_up": bell_draw(splits[1], (LAYERS, 2, NPTS, NPTS), (2 * NPTS + NPTS // 8) ** -0.5, 0.09375, ((0, 32), (2, 8))),
        "source_down": bell_draw(splits[2], (LAYERS, 2, SHOTS, NPTS), 0.3, 2.0, ((0, 32), (3, 8))),
        "source_up": bell_draw(splits[3], (LAYERS, 2, SHOTS, NPTS), 0.3, 2.0, ((0, 32), (3, 8))),
    }


def complex_apply(matrix, traces):
    real_part = jnp.dot(traces[0], matrix[0].T, preferred_element_type=jnp.float32) - jnp.dot(traces[1], matrix[1].T, preferred_element_type=jnp.float32)
    imag_part = jnp.dot(traces[0], matrix[1].T, preferred_element_type=jnp.float32) + jnp.dot(traces[1], matrix[0].T, preferred_element_type=jnp.float32)
    return jnp.stack([real_part, imag_part])


def sweep_step(state, inputs):
    matrix, source = inputs
    fresh = (complex_apply(matrix, state) + source.astype(jnp.float32)).astype(jnp.bfloat16)
    return fresh, fresh


def reference(green_down, green_up, source_down, source_up):
    initial = jnp.zeros((2, SHOTS, NPTS), jnp.bfloat16)
    final_down, down_traces = lax.scan(sweep_step, initial, (green_down, source_down))
    final_up, up_traces = lax.scan(sweep_step, initial, (green_up, source_up), reverse=True)
    return down_traces, up_traces
```

```python
import functools

import jax
import jax.numpy as jnp
from jax import lax
from jax.experimental import pallas as pl
from jax.experimental.pallas import tpu as pltpu
from jax.sharding import PartitionSpec as P

MESH = pl.DeviceIdType.MESH
LAYERS = 32
Y = 4
ROWS = 256
PIECE = 2 * ROWS
BATCHES = 12
LAG = 5


def kernel(
    batches, gd_ref, gu_ref, sd_ref, su_ref, o_ref,
    graw, gt, src, ins, outs,
    g_sem, gt_send, gt_recv, src_send, src_recv, send_sem, recv_sem, half_send, half_recv, o_sem,
):
    shots = sd_ref.shape[2]
    width = shots // batches
    layer = lax.axis_index("layer")
    iface = lax.axis_index("iface")
    y, core = iface // 2, lax.rem(iface, 2)
    sibling = (layer, 2 * y + 1 - core)
    first = jnp.where(layer < LAYERS // 2, 0, 1)
    second = 1 - first

    def load(d):
        def start(ref, at):
            pltpu.make_async_copy(ref.at[0], graw.at[at], g_sem.at[at]).start()

        @pl.when(d == 0)
        def _():
            start(gd_ref, 0)

        @pl.when(d == 1)
        def _():
            start(gu_ref, 1)

    def load_wait(d):
        pltpu.make_async_copy(gd_ref.at[0], graw.at[d], g_sem.at[d]).wait()

    def place_source(c):
        for d, ref in ((0, sd_ref), (1, su_ref)):
            for b in range(batches):
                rows = [ref[0, p, b * width : (b + 1) * width, :].astype(jnp.float32) for p in range(2)]
                src[d, b, :, c * ROWS : (c + 1) * ROWS] = jnp.concatenate(rows, 0).astype(jnp.bfloat16)

    def transpose(d, p, q, c):
        block = graw[d, p, :, pl.ds(pl.multiple_of(q * PIECE, PIECE), PIECE)]
        gt[d, q, :, p * PIECE + c * ROWS : p * PIECE + (c + 1) * ROWS] = block.T

    def gt_copy(d, p, q):
        cols = pl.ds(p * PIECE, ROWS)
        return pltpu.make_async_remote_copy(
            gt.at[d, q, :, cols], gt.at[d, q, :, cols], gt_send.at[d, p, q], gt_recv.at[d, p, q],
            device_id=sibling, device_id_type=MESH,
        )

    def src_copy(d):
        half = src.at[d, :, :, pl.ds(0, ROWS)]
        return pltpu.make_async_remote_copy(
            half, half, src_send.at[d], src_recv.at[d], device_id=sibling, device_id_type=MESH
        )

    def half_copy(d, b):
        half = outs.at[d, b, :, pl.ds(0, ROWS)]
        return pltpu.make_async_remote_copy(
            half, half, half_send.at[d, b], half_recv.at[d, b], device_id=sibling, device_id_type=MESH
        )

    def out_copy(d, b, c):
        return pltpu.make_async_copy(outs.at[d, b, :, pl.ds(c * ROWS, ROWS)], o_ref.at[d, b], o_sem.at[d, b])

    middle = (layer == LAYERS // 2 - 1) | (layer == LAYERS // 2)
    lead = jnp.where(middle, LAG, batches)

    def item(k):
        j = k - lead
        mixed = 2 * (batches - lead)
        in_lead, in_mixed = k < lead, j < mixed
        odd = lax.rem(jnp.maximum(j, 0), 2)
        half = jnp.maximum(j, 0) // 2
        d = jnp.where(in_lead, first, jnp.where(in_mixed, jnp.where(odd == 1, first, second), second))
        b = jnp.where(in_lead, k, jnp.where(in_mixed, jnp.where(odd == 1, lead + half, half), k - batches))
        return d, b

    load(first)
    load(second)
    barrier = pltpu.get_barrier_semaphore()
    pl.semaphore_signal(barrier, 1, device_id=sibling, device_id_type=MESH)

    @pl.when(core == 0)
    def _():
        place_source(0)
        pl.semaphore_wait(barrier, 1)
        src_copy(0).start()
        src_copy(1).start()
        for d in (first, second):
            load_wait(d)
            for p in range(2):

                def step(q, carry):
                    transpose(d, p, q, 0)
                    gt_copy(d, p, q).start()
                    return carry

                lax.fori_loop(0, Y, step, 0)

        def sent(k, carry):
            d, b = item(k)
            half_copy(d, b).wait_recv()
            out_copy(d, b, 0).start()
            return carry

        lax.fori_loop(0, 2 * batches, sent, 0)
        for d in range(2):
            src_copy(d).wait_send()
            for p in range(2):
                for q in range(Y):
                    gt_copy(d, p, q).wait_send()

        def written(k, carry):
            d, b = item(k)
            out_copy(d, b, 0).wait()
            return carry

        lax.fori_loop(0, 2 * batches, written, 0)

    @pl.when(core == 1)
    def _():
        above, below = lax.rem(layer + LAYERS - 1, LAYERS), lax.rem(layer + 1, LAYERS)
        for other in (above, below):
            for q in range(Y):
                pl.semaphore_signal(barrier, 1, device_id=(other, 2 * q + 1), device_id_type=MESH)
        place_source(1)
        pl.semaphore_wait(barrier, 1 + 2 * Y)
        src_copy(0).wait_recv()
        src_copy(1).wait_recv()

        def position(d):
            return jnp.where(d == 0, layer, LAYERS - 1 - layer)

        def prepare(d):
            load_wait(d)
            for p in range(2):

                def step(q, carry):
                    transpose(d, p, q, 1)
                    return carry

                lax.fori_loop(0, Y, step, 0)
            for p in range(2):
                for q in range(Y):
                    gt_copy(d, p, q).wait_recv()

        def send(d, b, off):
            to = (jnp.where(d == 0, below, above), 2 * lax.rem(y + off, Y) + 1)
            return pltpu.make_async_remote_copy(
                outs.at[d, b], ins.at[d, b, y], send_sem.at[d, b, off], recv_sem.at[d, b, y],
                device_id=to, device_id_type=MESH,
            )

        def arrival(d, b, q):
            return pltpu.make_async_remote_copy(
                outs.at[d, b], ins.at[d, b, q], send_sem.at[d, b, 0], recv_sem.at[d, b, q],
                device_id=sibling, device_id_type=MESH,
            )

        edge = (layer == 0) | (layer == LAYERS - 1)
        late = jnp.where((layer < LAYERS // 4) | (layer >= LAYERS - LAYERS // 4), batches, 0)

        @pl.when(jnp.logical_not(edge))
        def _():
            prepare(first)

        def step(k, carry):
            d, b = item(k)
            pos = position(d)

            @pl.when(k == late)
            def _():
                prepare(second)

            @pl.when(pos == 0)
            def _():
                outs[d, b] = src[d, b]

            @pl.when(pos > 0)
            def _():
                total = None
                for off in (0, 1, 3, 2):
                    q = lax.rem(y + off, Y)
                    arrival(d, b, q).wait_recv()
                    part = jnp.dot(ins[d, b, q], gt[d, q], preferred_element_type=jnp.float32)
                    total = part if total is None else total + part
                real = total[:width, :PIECE] - total[width:, PIECE:]
                imag = total[:width, PIECE:] + total[width:, :PIECE]
                fresh = jnp.concatenate([real, imag], 0) + src[d, b].astype(jnp.float32)
                outs[d, b] = fresh.astype(jnp.bfloat16)

            @pl.when(pos < LAYERS - 1)
            def _():
                for off in (2, 1, 3, 0):
                    send(d, b, off).start()

            half_copy(d, b).start()
            out_copy(d, b, 1).start()
            return carry

        lax.fori_loop(0, 2 * batches, step, 0)

        @pl.when(edge)
        def _():
            prepare(first)

        def finish(k, carry):
            d, b = item(k)

            @pl.when(position(d) < LAYERS - 1)
            def _():
                for off in range(Y):
                    send(d, b, off).wait_send()

            half_copy(d, b).wait_send()
            out_copy(d, b, 1).wait()
            return carry

        lax.fori_loop(0, 2 * batches, finish, 0)


def on_device(green_down, green_up, source_down, source_up):
    shots = source_down.shape[2]
    width = shots // BATCHES
    points = green_down.shape[3]
    any_space = pl.BlockSpec(memory_space=pl.ANY)
    vmem = pl.BlockSpec(memory_space=pltpu.VMEM)
    dma = pltpu.SemaphoreType.DMA
    out = pl.pallas_call(
        functools.partial(kernel, BATCHES),
        out_shape=jax.ShapeDtypeStruct((2, BATCHES, 2 * width, ROWS), jnp.bfloat16),
        in_specs=[any_space, any_space, vmem, vmem],
        out_specs=any_space,
        scratch_shapes=[
            pltpu.VMEM((2, 2, ROWS, points), jnp.bfloat16),
            pltpu.VMEM((2, Y, PIECE, 2 * PIECE), jnp.bfloat16),
            pltpu.VMEM((2, BATCHES, 2 * width, PIECE), jnp.bfloat16),
            pltpu.VMEM((2, BATCHES, Y, 2 * width, PIECE), jnp.bfloat16),
            pltpu.VMEM((2, BATCHES, 2 * width, PIECE), jnp.bfloat16),
            dma((2,)),
            dma((2, 2, Y)),
            dma((2, 2, Y)),
            dma((2,)),
            dma((2,)),
            dma((2, BATCHES, Y)),
            dma((2, BATCHES, Y)),
            dma((2, BATCHES)),
            dma((2, BATCHES)),
            dma((2, BATCHES)),
        ],
        compiler_params=pltpu.CompilerParams(
            collective_id=0, has_side_effects=True, vmem_limit_bytes=40 << 20
        ),
    )(green_down, green_up, source_down, source_up)
    out = out.reshape(2, BATCHES, 2, width, ROWS).transpose(0, 2, 1, 3, 4).reshape(2, 2, shots, ROWS)
    return out[0][None], out[1][None]


def solution(mesh):
    in_specs = (
        P("layer", None, "iface", None),
        P("layer", None, "iface", None),
        P("layer", None, None, "iface"),
        P("layer", None, None, "iface"),
    )
    out_specs = (P("layer", None, None, "iface"), P("layer", None, None, "iface"))
    return jax.shard_map(
        on_device, mesh=mesh, in_specs=in_specs, out_specs=out_specs, check_vma=False
    )
```

```python
import functools

import jax
import jax.numpy as jnp
from jax import lax
from jax.experimental import pallas as pl
from jax.experimental.pallas import tpu as pltpu
from jax.sharding import PartitionSpec as P

MESH = pl.DeviceIdType.MESH
LAYERS = 32
Y = 4
ROWS = 256
PIECE = 2 * ROWS
SIDE = 256
BATCHES = 12
LAG = 8


def kernel(
    batches, gd_ref, gu_ref, sd_ref, su_ref, o_ref,
    graw, gt, src, ins, outs,
    g_sem, gt_send, gt_recv, src_send, src_recv, send_sem, recv_sem, half_send, half_recv, o_sem,
):
    shots = sd_ref.shape[2]
    width = shots // batches
    layer = lax.axis_index("layer")
    iface = lax.axis_index("iface")
    y, core = iface // 2, lax.rem(iface, 2)
    sibling = (layer, 2 * y + 1 - core)
    first = jnp.where(layer < LAYERS // 2, 0, 1)
    second = 1 - first

    def load(d):
        def start(ref, at):
            pltpu.make_async_copy(ref.at[0], graw.at[at], g_sem.at[at]).start()

        @pl.when(d == 0)
        def _():
            start(gd_ref, 0)

        @pl.when(d == 1)
        def _():
            start(gu_ref, 1)

    def load_wait(d):
        pltpu.make_async_copy(gd_ref.at[0], graw.at[d], g_sem.at[d]).wait()

    def place_source(c):
        for d, ref in ((0, sd_ref), (1, su_ref)):
            for b in range(batches):
                rows = [ref[0, p, b * width : (b + 1) * width, :].astype(jnp.float32) for p in range(2)]
                src[d, b, :, c * ROWS : (c + 1) * ROWS] = jnp.concatenate(rows, 0).astype(jnp.bfloat16)

    def transpose(d, p, q, c):
        block = graw[d, p, :, pl.ds(pl.multiple_of(q * PIECE, PIECE), PIECE)]
        gt[d, q, :, p * PIECE + c * ROWS : p * PIECE + (c + 1) * ROWS] = block.T

    def gt_copy(d, p, q):
        cols = pl.ds(p * PIECE, ROWS)
        return pltpu.make_async_remote_copy(
            gt.at[d, q, :, cols], gt.at[d, q, :, cols], gt_send.at[d, p, q], gt_recv.at[d, p, q],
            device_id=sibling, device_id_type=MESH,
        )

    def src_copy(d):
        half = src.at[d, :, :, pl.ds(0, ROWS)]
        return pltpu.make_async_remote_copy(
            half, half, src_send.at[d], src_recv.at[d], device_id=sibling, device_id_type=MESH
        )

    def half_copy(d, b):
        half = outs.at[d, b, :, pl.ds(0, ROWS)]
        return pltpu.make_async_remote_copy(
            half, half, half_send.at[d, b], half_recv.at[d, b], device_id=sibling, device_id_type=MESH
        )

    def out_copy(d, b, c):
        return pltpu.make_async_copy(outs.at[d, b, :, pl.ds(c * ROWS, ROWS)], o_ref.at[d, b], o_sem.at[d, b])

    middle = (layer == LAYERS // 2 - 1) | (layer == LAYERS // 2)
    lead = jnp.where(middle, LAG, batches)

    def item(k):
        j = k - lead
        mixed = 2 * (batches - lead)
        in_lead, in_mixed = k < lead, j < mixed
        odd = lax.rem(jnp.maximum(j, 0), 2)
        half = jnp.maximum(j, 0) // 2
        d = jnp.where(in_lead, first, jnp.where(in_mixed, jnp.where(odd == 1, first, second), second))
        b = jnp.where(in_lead, k, jnp.where(in_mixed, jnp.where(odd == 1, lead + half, half), k - batches))
        return d, b

    load(first)
    load(second)
    barrier = pltpu.get_barrier_semaphore()
    pl.semaphore_signal(barrier, 1, device_id=sibling, device_id_type=MESH)

    @pl.when(core == 0)
    def _():
        place_source(0)
        pl.semaphore_wait(barrier, 1)
        src_copy(0).start()
        src_copy(1).start()
        for d in (first, second):
            load_wait(d)
            for p in range(2):

                def step(q, carry):
                    transpose(d, p, q, 0)
                    gt_copy(d, p, q).start()
                    return carry

                lax.fori_loop(0, Y, step, 0)

        def sent(k, carry):
            d, b = item(k)
            half_copy(d, b).wait_recv()
            out_copy(d, b, 0).start()
            return carry

        lax.fori_loop(0, 2 * batches, sent, 0)
        for d in range(2):
            src_copy(d).wait_send()
            for p in range(2):
                for q in range(Y):
                    gt_copy(d, p, q).wait_send()

        def written(k, carry):
            d, b = item(k)
            out_copy(d, b, 0).wait()
            return carry

        lax.fori_loop(0, 2 * batches, written, 0)

    @pl.when(core == 1)
    def _():
        above, below = lax.rem(layer + LAYERS - 1, LAYERS), lax.rem(layer + 1, LAYERS)
        for other in (above, below):
            for q in range(Y):
                pl.semaphore_signal(barrier, 1, device_id=(other, 2 * q + 1), device_id_type=MESH)
        place_source(1)
        pl.semaphore_wait(barrier, 1 + 2 * Y)
        src_copy(0).wait_recv()
        src_copy(1).wait_recv()

        def position(d):
            return jnp.where(d == 0, layer, LAYERS - 1 - layer)

        def prepare(d):
            load_wait(d)
            for p in range(2):

                def step(q, carry):
                    transpose(d, p, q, 1)
                    return carry

                lax.fori_loop(0, Y, step, 0)
            for p in range(2):
                for q in range(Y):
                    gt_copy(d, p, q).wait_recv()

        def send(d, b, off):
            to = (jnp.where(d == 0, below, above), 2 * lax.rem(y + off, Y) + 1)
            return pltpu.make_async_remote_copy(
                outs.at[d, b], ins.at[d, b, y], send_sem.at[d, b, off], recv_sem.at[d, b, y],
                device_id=to, device_id_type=MESH,
            )

        def arrival(d, b, q):
            return pltpu.make_async_remote_copy(
                outs.at[d, b], ins.at[d, b, q], send_sem.at[d, b, 0], recv_sem.at[d, b, q],
                device_id=sibling, device_id_type=MESH,
            )

        edge = (layer == 0) | (layer == LAYERS - 1)
        late = jnp.where((layer < LAYERS // 4) | (layer >= LAYERS - LAYERS // 4), batches, 0)

        @pl.when(jnp.logical_not(edge))
        def _():
            prepare(first)

        def step(k, carry):
            d, b = item(k)
            pos = position(d)

            @pl.when(k == late)
            def _():
                prepare(second)

            @pl.when(edge & (k == late))
            def _():
                load_wait(first)
                for p in range(2):
                    for q in range(Y):
                        gt_copy(first, p, q).wait_recv()

            @pl.when(pos == 0)
            def _():
                outs[d, b] = src[d, b]

            @pl.when(pos > 0)
            def _():
                def run(*sums):
                    order = [lax.rem(y + off, Y) for off in (0, 1, 3, 2)]

                    def push(q, t):
                        rows = slice(t // 2 * SIDE, (t // 2 + 1) * SIDE)
                        for m in range(2):
                            at = (2 * m + t % 2) * SIDE
                            pltpu.matmul_push_rhs(gt[d, q, rows, at : at + SIDE], t % 2, m)

                    def multiply(block, t):
                        cols = slice(t // 2 * SIDE, (t // 2 + 1) * SIDE)
                        for m in range(2):
                            pltpu.matmul_acc_lhs(sums[2 * m + t % 2], block[:, cols], t % 2)

                    push(order[0], 0)
                    push(order[0], 1)
                    for n, q in enumerate(order):
                        arrival(d, b, q).wait_recv()
                        block = ins[d, b, q]
                        for t in range(4):
                            multiply(block, t)
                            if t < 2:
                                push(q, t + 2)
                            elif n + 1 < Y:
                                push(order[n + 1], t - 2)
                    for h in range(2):
                        by_real, by_imag = pltpu.matmul_pop(sums[h]), pltpu.matmul_pop(sums[2 + h])
                        real = by_real[:width] - by_imag[width:]
                        imag = by_imag[:width] + by_real[width:]
                        cols = slice(h * SIDE, (h + 1) * SIDE)
                        fresh = jnp.concatenate([real, imag], 0) + src[d, b, :, cols].astype(jnp.float32)
                        outs[d, b, :, cols] = fresh.astype(jnp.bfloat16)

                scratch = [pltpu.ACC(mxu_id=n // 2)((2 * width, SIDE), jnp.float32) for n in range(4)]
                pl.run_scoped(run, *scratch)

            @pl.when(pos < LAYERS - 1)
            def _():
                for off in (2, 1, 3, 0):
                    send(d, b, off).start()

            half_copy(d, b).start()
            out_copy(d, b, 1).start()
            return carry

        lax.fori_loop(0, 2 * batches, step, 0)

        def finish(k, carry):
            d, b = item(k)

            @pl.when(position(d) < LAYERS - 1)
            def _():
                for off in range(Y):
                    send(d, b, off).wait_send()

            half_copy(d, b).wait_send()
            out_copy(d, b, 1).wait()
            return carry

        lax.fori_loop(0, 2 * batches, finish, 0)


def on_device(green_down, green_up, source_down, source_up):
    shots = source_down.shape[2]
    width = shots // BATCHES
    points = green_down.shape[3]
    any_space = pl.BlockSpec(memory_space=pl.ANY)
    vmem = pl.BlockSpec(memory_space=pltpu.VMEM)
    dma = pltpu.SemaphoreType.DMA
    out = pl.pallas_call(
        functools.partial(kernel, BATCHES),
        out_shape=jax.ShapeDtypeStruct((2, BATCHES, 2 * width, ROWS), jnp.bfloat16),
        in_specs=[any_space, any_space, vmem, vmem],
        out_specs=any_space,
        scratch_shapes=[
            pltpu.VMEM((2, 2, ROWS, points), jnp.bfloat16),
            pltpu.VMEM((2, Y, PIECE, 2 * PIECE), jnp.bfloat16),
            pltpu.VMEM((2, BATCHES, 2 * width, PIECE), jnp.bfloat16),
            pltpu.VMEM((2, BATCHES, Y, 2 * width, PIECE), jnp.bfloat16),
            pltpu.VMEM((2, BATCHES, 2 * width, PIECE), jnp.bfloat16),
            dma((2,)),
            dma((2, 2, Y)),
            dma((2, 2, Y)),
            dma((2,)),
            dma((2,)),
            dma((2, BATCHES, Y)),
            dma((2, BATCHES, Y)),
            dma((2, BATCHES)),
            dma((2, BATCHES)),
            dma((2, BATCHES)),
        ],
        compiler_params=pltpu.CompilerParams(
            collective_id=0, has_side_effects=True, vmem_limit_bytes=60 << 20
        ),
    )(green_down, green_up, source_down, source_up)
    out = out.reshape(2, BATCHES, 2, width, ROWS).transpose(0, 2, 1, 3, 4).reshape(2, 2, shots, ROWS)
    return out[0][None], out[1][None]


def solution(mesh):
    in_specs = (
        P("layer", None, "iface", None),
        P("layer", None, "iface", None),
        P("layer", None, None, "iface"),
        P("layer", None, None, "iface"),
    )
    out_specs = (P("layer", None, None, "iface"), P("layer", None, None, "iface"))
    return jax.shard_map(
        on_device, mesh=mesh, in_specs=in_specs, out_specs=out_specs, check_vma=False
    )
```

```python
import functools

import jax
import jax.numpy as jnp
from jax import lax
from jax.experimental import pallas as pl
from jax.experimental.pallas import tpu as pltpu
from jax.sharding import PartitionSpec as P

MESH = pl.DeviceIdType.MESH
LAYERS = 32
LAST = LAYERS - 1
MID = LAYERS // 2
Y = 4
ROWS = 256
PIECE = 2 * ROWS
SIDE = 256
BATCHES = 12
SENDS = Y + 1


def kernel(
    batches, gd_ref, gu_ref, sd_ref, su_ref, o_ref,
    graw, sraw, gt, src, ins, outs,
    g_sem, s_sem, gt_send, gt_recv, src_send, src_recv, send_sem, recv_sem, half_send, half_recv, o_sem,
):
    shots = sd_ref.shape[2]
    width = shots // batches
    layer = lax.axis_index("layer")
    iface = lax.axis_index("iface")
    y, core = iface // 2, lax.rem(iface, 2)
    sibling = (layer, 2 * y + 1 - core)
    first = jnp.where(layer < MID, 0, 1)
    second = 1 - first
    middle = (layer == MID - 1) | (layer == MID)
    central = (layer >= MID // 2) & (layer < LAYERS - MID // 2)

    def worker_of(at, d):
        return jnp.where(((at == MID - 1) | (at == MID)) & (d == 0), 0, 1)

    def position(d):
        return jnp.where(d == 0, layer, LAST - layer)

    def load(d):
        def start(ref, at):
            for p in range(2):
                pltpu.make_async_copy(ref.at[0, p], graw.at[at, p], g_sem.at[at, p]).start()

        @pl.when(d == 0)
        def _():
            start(gd_ref, 0)

        @pl.when(d == 1)
        def _():
            start(gu_ref, 1)

    def load_wait(d, p):
        pltpu.make_async_copy(gd_ref.at[0, p], graw.at[d, p], g_sem.at[d, p]).wait()

    def source_load(d):
        ref = (sd_ref, su_ref)[d]
        return pltpu.make_async_copy(ref.at[0], sraw.at[d], s_sem.at[d])

    def place_source(c):
        for d in range(2):
            source_load(d).wait()
            for b in range(batches):
                rows = [sraw[d, p, b * width : (b + 1) * width, :].astype(jnp.float32) for p in range(2)]
                src[d, b, :, c * ROWS : (c + 1) * ROWS] = jnp.concatenate(rows, 0).astype(jnp.bfloat16)

    def transpose(d, c, then=None):
        for p in range(2):
            load_wait(d, p)

            def step(q, carry):
                block = graw[d, p, :, pl.ds(pl.multiple_of(q * PIECE, PIECE), PIECE)]
                gt[d, q, :, p * PIECE + c * ROWS : p * PIECE + (c + 1) * ROWS] = block.T
                if then is not None:
                    then(p, q)
                return carry

            lax.fori_loop(0, Y, step, 0)

    def remote(a, b, send, recv, to):
        return pltpu.make_async_remote_copy(a, b, send, recv, device_id=to, device_id_type=MESH)

    def gt_copy(d, c, p, q):
        half = gt.at[d, q, :, pl.ds(p * PIECE + c * ROWS, ROWS)]
        return remote(half, half, gt_send.at[d, p, q], gt_recv.at[d, p, q], sibling)

    def for_gt(act, d, c):
        for p in range(2):
            for q in range(Y):
                act(gt_copy(d, c, p, q))

    def src_copy(d, c):
        half = src.at[d, :, :, pl.ds(c * ROWS, ROWS)]
        return remote(half, half, src_send.at[d], src_recv.at[d], sibling)

    def half_copy(d, b, c):
        half = outs.at[d, b, :, pl.ds((1 - c) * ROWS, ROWS)]
        return remote(half, o_ref.at[d, b], half_send.at[d, b], half_recv.at[d, b], sibling)

    def out_copy(d, b, c):
        return pltpu.make_async_copy(outs.at[d, b, :, pl.ds(c * ROWS, ROWS)], o_ref.at[d, b], o_sem.at[d, b])

    barrier = pltpu.get_barrier_semaphore()

    def greet(at, c):
        for q in range(Y):
            pl.semaphore_signal(barrier, 1, device_id=(at, 2 * q + c), device_id_type=MESH)

    def targets(d):
        at = jnp.where(d == 0, layer + 1, layer - 1)
        worker = worker_of(at, d)
        return [(at, 2 * lax.rem(y + off, Y) + worker) for off in range(Y)]

    def send(d, b, kind, to):
        off = 2 if kind == Y else kind
        a, z = outs.at[d, b], ins.at[d, b, y]
        if off == 2:
            cols = pl.ds(SIDE if kind == Y else 0, SIDE)
            a, z = outs.at[d, b, :, cols], ins.at[d, b, y, :, cols]
        return remote(a, z, send_sem.at[d, b, kind], recv_sem.at[d, b, kind], to[off])

    def work(c, begin, end):
        def mine(d):
            return worker_of(layer, d) == c

        for d in (first, second):

            @pl.when(mine(d))
            def _():
                src_copy(d, 1 - c).wait_recv()

        @pl.when(mine(first) & (position(first) > 0))
        def _():
            for_gt(lambda copy: copy.wait_recv(), first, 1 - c)

        def drain(d):
            def step(b, carry):
                @pl.when(position(d) < LAST)
                def _():
                    for kind in range(SENDS):
                        send(d, b, kind, targets(d)).wait_send()

                half_copy(d, b, c).wait_send()
                out_copy(d, b, c).wait()
                return carry

            lax.fori_loop(0, batches, step, 0)

        def step(k, carry):
            d = jnp.where(k < batches, first, second)
            b = lax.rem(k, batches)
            pos = position(d)
            to = targets(d)

            def send_all():
                for kind in (2, Y, 1, 3, 0):
                    send(d, b, kind, to).start()

            @pl.when(k == batches)
            def _():
                if c == 1:

                    @pl.when(jnp.logical_not(central))
                    def _():
                        transpose(second, c)

                    @pl.when(begin == 0)
                    def _():
                        drain(first)

                for_gt(lambda copy: copy.wait_recv(), second, 1 - c)

            @pl.when(pos == 0)
            def _():
                outs[d, b] = src[d, b]
                send_all()

            def run(*sums):
                order = [lax.rem(y + off, Y) for off in (0, 1, 3, 2)]
                kinds = (0, 3, 1, 2)

                def push(q, t):
                    rows = slice(t // 2 * SIDE, (t // 2 + 1) * SIDE)
                    for m in range(2):
                        at = (2 * m + t % 2) * SIDE
                        pltpu.matmul_push_rhs(gt[d, q, rows, at : at + SIDE], t % 2, m)

                def arrive(n, kind):
                    part = (d, b, order[n])
                    ref = ins.at[part]
                    if kind in (2, Y):
                        ref = ins.at[(*part, slice(None), pl.ds(SIDE if kind == Y else 0, SIDE))]
                    remote(ref, ref, send_sem.at[d, b, kind], recv_sem.at[d, b, kind], sibling).wait_recv()

                push(order[0], 0)
                push(order[0], 1)
                for n, q in enumerate(order):
                    arrive(n, kinds[n])
                    for t in range(4):
                        if t == 2 and kinds[n] == 2:
                            arrive(n, Y)
                        if t % 2 == 0:
                            block = ins[d, b, q, :, t // 2 * SIDE : (t // 2 + 1) * SIDE]
                        for m in range(2):
                            pltpu.matmul_acc_lhs(sums[2 * m + t % 2], block, t % 2)
                        if t < 2:
                            push(q, t + 2)
                        elif n + 1 < Y:
                            push(order[n + 1], t - 2)
                for h in range(2):
                    by_real, by_imag = pltpu.matmul_pop(sums[h]), pltpu.matmul_pop(sums[2 + h])
                    real = by_real[:width] - by_imag[width:]
                    imag = by_imag[:width] + by_real[width:]
                    cols = slice(h * SIDE, (h + 1) * SIDE)
                    fresh = jnp.concatenate([real, imag], 0) + src[d, b, :, cols].astype(jnp.float32)
                    outs[d, b, :, cols] = fresh.astype(jnp.bfloat16)

            def compute():
                sums = [pltpu.ACC(mxu_id=n // 2)((2 * width, SIDE), jnp.float32) for n in range(4)]
                pl.run_scoped(run, *sums)

            @pl.when((pos > 0) & (pos < LAST))
            def _():
                compute()
                send_all()

            @pl.when(pos == LAST)
            def _():
                compute()

            half_copy(d, b, c).start()
            out_copy(d, b, c).start()
            return carry

        lax.fori_loop(begin, end, step, 0)
        drain(jnp.where(end == batches, first, second))

    def serve(c):
        def helps(d):
            return worker_of(layer, d) != c

        def before():
            for d in (first, second):

                @pl.when(helps(d))
                def _():
                    src_copy(d, c).start()

        def offer(d):
            def then(p, q):
                @pl.when(helps(d))
                def _():
                    gt_copy(d, c, p, q).start()

            transpose(d, c, then)

        def after():
            for d in (first, second):

                @pl.when(helps(d))
                def _():
                    def step(b, carry):
                        half_copy(d, b, 1 - c).wait_recv()
                        return carry

                    src_copy(d, c).wait_send()

                    @pl.when(position(d) > 0)
                    def _():
                        for_gt(lambda copy: copy.wait_send(), d, c)

                    lax.fori_loop(0, batches, step, 0)

        return before, offer, after

    for d in range(2):
        source_load(d).start()
    load(first)
    pl.semaphore_signal(barrier, 1, device_id=sibling, device_id_type=MESH)

    def skip(d):
        for p in range(2):
            load_wait(d, p)

    @pl.when(core == 0)
    def _():
        before, offer, after = serve(0)

        @pl.when(middle)
        def _():
            for hop in (-1, 1):
                greet(layer + hop, worker_of(layer + hop, 0))

        load(second)
        place_source(0)
        pl.semaphore_wait(barrier, 1 + jnp.where(middle, 2 * Y, 0))
        before()

        @pl.when(position(first) > 0)
        def _():
            offer(first)

        @pl.when(position(first) == 0)
        def _():
            skip(first)

        offer(second)

        @pl.when(middle)
        def _():
            begin = jnp.where(first == 0, 0, batches)
            work(0, begin, begin + batches)

        after()

    @pl.when(core == 1)
    def _():
        before, offer, after = serve(1)
        guests = 0
        for hop in (-1, 1):
            inside = (layer + hop >= 0) & (layer + hop <= LAST)
            guests = guests + jnp.where(inside, Y, 0)

            @pl.when(inside)
            def _():
                greet(layer + hop, 1)

        near = (layer == MID - 2) | (layer == MID + 1)
        guests = guests + jnp.where(near, Y, 0)

        @pl.when(near)
        def _():
            greet(jnp.where(layer < MID, MID - 1, MID), 0)

        load(second)
        place_source(1)

        @pl.when((position(first) > 0) & jnp.logical_not(middle))
        def _():
            transpose(first, 1)

        @pl.when(position(first) == 0)
        def _():
            skip(first)

        pl.semaphore_wait(barrier, 1 + guests)
        before()

        @pl.when(middle)
        def _():
            offer(first)

        @pl.when(central)
        def _():
            offer(second)

        begin = jnp.where(middle & (first == 0), batches, 0)
        work(1, begin, jnp.where(middle & (first == 1), batches, 2 * batches))
        after()


def on_device(green_down, green_up, source_down, source_up):
    shots = source_down.shape[2]
    width = shots // BATCHES
    points = green_down.shape[3]
    any_space = pl.BlockSpec(memory_space=pl.ANY)
    dma = pltpu.SemaphoreType.DMA
    trace = (BATCHES, 2 * width, PIECE)
    out = pl.pallas_call(
        functools.partial(kernel, BATCHES),
        out_shape=jax.ShapeDtypeStruct((2, BATCHES, 2 * width, ROWS), jnp.bfloat16),
        in_specs=[any_space] * 4,
        out_specs=any_space,
        scratch_shapes=[
            pltpu.VMEM((2, 2, ROWS, points), jnp.bfloat16),
            pltpu.VMEM((2, 2, shots, ROWS), jnp.bfloat16),
            pltpu.VMEM((2, Y, PIECE, 2 * PIECE), jnp.bfloat16),
            pltpu.VMEM((2, *trace), jnp.bfloat16),
            pltpu.VMEM((2, BATCHES, Y, 2 * width, PIECE), jnp.bfloat16),
            pltpu.VMEM((2, *trace), jnp.bfloat16),
            dma((2, 2)),
            dma((2,)),
            dma((2, 2, Y)),
            dma((2, 2, Y)),
            dma((2,)),
            dma((2,)),
            dma((2, BATCHES, SENDS)),
            dma((2, BATCHES, SENDS)),
            dma((2, BATCHES)),
            dma((2, BATCHES)),
            dma((2, BATCHES)),
        ],
        compiler_params=pltpu.CompilerParams(
            collective_id=0, has_side_effects=True, vmem_limit_bytes=60 << 20
        ),
    )(green_down, green_up, source_down, source_up)
    out = out.reshape(2, BATCHES, 2, width, ROWS).transpose(0, 2, 1, 3, 4).reshape(2, 2, shots, ROWS)
    return out[0][None], out[1][None]


def solution(mesh):
    in_specs = (
        P("layer", None, "iface", None),
        P("layer", None, "iface", None),
        P("layer", None, None, "iface"),
        P("layer", None, None, "iface"),
    )
    out_specs = (P("layer", None, None, "iface"), P("layer", None, None, "iface"))
    return jax.shard_map(
        on_device, mesh=mesh, in_specs=in_specs, out_specs=out_specs, check_vma=False
    )
```

```python
import functools

import jax
import jax.numpy as jnp
from jax import lax
from jax.experimental import pallas as pl
from jax.experimental.pallas import tpu as pltpu
from jax.sharding import PartitionSpec as P

MESH = pl.DeviceIdType.MESH
LAYERS = 32
LAST = LAYERS - 1
MID = LAYERS // 2
Y = 4
ROWS = 256
PIECE = 2 * ROWS
SIDE = 256
BATCHES = 12
SENDS = Y + 1


def kernel(
    batches, gd_ref, gu_ref, sd_ref, su_ref, o_ref,
    graw, sraw, gt, src, ins, outs,
    g_sem, s_sem, gt_send, gt_recv, src_send, src_recv, send_sem, recv_sem, half_send, half_recv, o_sem,
    swap_send, swap_recv, swap_src,
):
    shots = sd_ref.shape[2]
    width = shots // batches
    layer = lax.axis_index("layer")
    iface = lax.axis_index("iface")
    y, core = iface // 2, lax.rem(iface, 2)
    sibling = (layer, 2 * y + 1 - core)
    first = jnp.where(layer < MID, 0, 1)
    second = 1 - first
    middle = (layer == MID - 1) | (layer == MID)
    central = (layer >= MID // 2) & (layer < LAYERS - MID // 2)

    def worker_of(at, d):
        return jnp.where(((at == MID - 1) | (at == MID)) & (d == 0), 0, 1)

    def flips(at, d):
        plane = at // Y
        return (d == 1) & ((plane == 1) | (plane == 3))

    def host(at, d):
        mirrored = at // Y * Y + Y - 1 - lax.rem(at, Y)
        return jnp.where(flips(at, d), mirrored, at)

    flipped = flips(layer, 1)
    partner = host(layer, 1)

    def position(d):
        return jnp.where(d == 0, layer, LAST - partner)

    def slot_of(d):
        return jnp.where(flipped & (d == 1), 2, d)

    def load(d):
        def start(ref, at):
            for p in range(2):
                pltpu.make_async_copy(ref.at[0, p], graw.at[at, p], g_sem.at[at, p]).start()

        @pl.when(d == 0)
        def _():
            start(gd_ref, 0)

        @pl.when(d == 1)
        def _():
            start(gu_ref, 1)

    def load_wait(d, p):
        pltpu.make_async_copy(gd_ref.at[0, p], graw.at[d, p], g_sem.at[d, p]).wait()

    def source_load(d):
        ref = (sd_ref, su_ref)[d]
        return pltpu.make_async_copy(ref.at[0], sraw.at[d], s_sem.at[d])

    def place_source(c):
        for d in range(2):
            source_load(d).wait()
            for b in range(batches):
                rows = [sraw[d, p, b * width : (b + 1) * width, :].astype(jnp.float32) for p in range(2)]
                src[d, b, :, c * ROWS : (c + 1) * ROWS] = jnp.concatenate(rows, 0).astype(jnp.bfloat16)

    def transpose(d, c, then=None):
        for p in range(2):
            load_wait(d, p)

            def step(q, carry):
                block = graw[d, p, :, pl.ds(pl.multiple_of(q * PIECE, PIECE), PIECE)]
                gt[d, q, :, p * PIECE + c * ROWS : p * PIECE + (c + 1) * ROWS] = block.T
                if then is not None:
                    then(p, q)
                return carry

            lax.fori_loop(0, Y, step, 0)

    def remote(a, b, send, recv, to):
        return pltpu.make_async_remote_copy(a, b, send, recv, device_id=to, device_id_type=MESH)

    def gt_copy(d, c, p, q):
        half = gt.at[d, q, :, pl.ds(p * PIECE + c * ROWS, ROWS)]
        return remote(half, half, gt_send.at[d, p, q], gt_recv.at[d, p, q], sibling)

    def for_gt(act, d, c):
        for p in range(2):
            for q in range(Y):
                act(gt_copy(d, c, p, q))

    def src_copy(d, c):
        half = src.at[d, :, :, pl.ds(c * ROWS, ROWS)]
        return remote(half, half, src_send.at[d], src_recv.at[d], sibling)

    def swap_copy(c, p, q):
        cols = pl.ds(p * PIECE + c * ROWS, ROWS)
        a, z = gt.at[1, q, :, cols], gt.at[2, q, :, cols]
        return remote(a, z, swap_send.at[p, q], swap_recv.at[c, p, q], (partner, 2 * y + 1))

    def swap_source(c):
        cols = pl.ds(c * ROWS, ROWS)
        a, z = src.at[1, :, :, cols], src.at[2, :, :, cols]
        return remote(a, z, swap_src.at[2], swap_src.at[c], (partner, 2 * y + 1))

    def swap_out(b, c):
        half = outs.at[1, b, :, pl.ds(c * ROWS, ROWS)]
        sem = (half_send, o_sem)[c].at[1, b]
        return remote(half, o_ref.at[1, b], sem, half_recv.at[1, b], (partner, 2 * y + c))

    def half_copy(d, b, c):
        half = outs.at[d, b, :, pl.ds((1 - c) * ROWS, ROWS)]
        return remote(half, o_ref.at[d, b], half_send.at[d, b], half_recv.at[d, b], sibling)

    def out_copy(d, b, c):
        return pltpu.make_async_copy(outs.at[d, b, :, pl.ds(c * ROWS, ROWS)], o_ref.at[d, b], o_sem.at[d, b])

    barrier = pltpu.get_barrier_semaphore()

    def greet(at, c):
        for q in range(Y):
            pl.semaphore_signal(barrier, 1, device_id=(at, 2 * q + c), device_id_type=MESH)

    def targets(d):
        at = jnp.where(d == 0, layer + 1, host(jnp.maximum(partner - 1, 0), 1))
        worker = worker_of(at, d)
        return [(at, 2 * lax.rem(y + off, Y) + worker) for off in range(Y)]

    def send(d, b, kind, to):
        off = 2 if kind == Y else kind
        a, z = outs.at[d, b], ins.at[d, b, y]
        if off == 2:
            cols = pl.ds(SIDE if kind == Y else 0, SIDE)
            a, z = outs.at[d, b, :, cols], ins.at[d, b, y, :, cols]
        return remote(a, z, send_sem.at[d, b, kind], recv_sem.at[d, b, kind], to[off])

    def work(c, begin, end):
        def mine(d):
            return worker_of(layer, d) == c

        for d in (first, second):

            @pl.when(mine(d) & (slot_of(d) < 2))
            def _():
                src_copy(d, 1 - c).wait_recv()

        @pl.when(mine(first) & (position(first) > 0))
        def _():
            for_gt(lambda copy: copy.wait_recv(), first, 1 - c)

        def drain(d):
            def step(b, carry):
                @pl.when(position(d) < LAST)
                def _():
                    for kind in range(SENDS):
                        send(d, b, kind, targets(d)).wait_send()

                if c == 1:

                    @pl.when(slot_of(d) == 2)
                    def _():
                        for at in range(2):
                            swap_out(b, at).wait_send()

                @pl.when(slot_of(d) < 2)
                def _():
                    half_copy(d, b, c).wait_send()
                    out_copy(d, b, c).wait()

                return carry

            lax.fori_loop(0, batches, step, 0)

        def step(k, carry):
            d = jnp.where(k < batches, first, second)
            b = lax.rem(k, batches)
            pos = position(d)
            slot = slot_of(d)
            to = targets(d)

            def send_all():
                for kind in (2, Y, 1, 3, 0):
                    send(d, b, kind, to).start()

            @pl.when(k == batches)
            def _():
                if c == 1:

                    @pl.when(jnp.logical_not(central))
                    def _():
                        def then(p, q):
                            @pl.when(flipped)
                            def _():
                                swap_copy(c, p, q).start()

                        transpose(second, c, then)

                    @pl.when(begin == 0)
                    def _():
                        drain(first)

                if c == 1:

                    @pl.when(flipped)
                    def _():
                        for at in range(2):
                            swap_source(at).wait_recv()
                            for p in range(2):
                                for q in range(Y):
                                    swap_copy(at, p, q).wait_recv()

                @pl.when(slot_of(second) < 2)
                def _():
                    for_gt(lambda copy: copy.wait_recv(), second, 1 - c)

            @pl.when(pos == 0)
            def _():
                outs[d, b] = src[d, b]
                send_all()

            def run(*sums):
                order = [lax.rem(y + off, Y) for off in (0, 1, 3, 2)]
                kinds = (0, 3, 1, 2)

                def push(q, t):
                    rows = slice(t // 2 * SIDE, (t // 2 + 1) * SIDE)
                    for m in range(2):
                        at = (2 * m + t % 2) * SIDE
                        pltpu.matmul_push_rhs(gt[slot, q, rows, at : at + SIDE], t % 2, m)

                def arrive(n, kind):
                    part = (d, b, order[n])
                    ref = ins.at[part]
                    if kind in (2, Y):
                        ref = ins.at[(*part, slice(None), pl.ds(SIDE if kind == Y else 0, SIDE))]
                    remote(ref, ref, send_sem.at[d, b, kind], recv_sem.at[d, b, kind], sibling).wait_recv()

                push(order[0], 0)
                push(order[0], 1)
                for n, q in enumerate(order):
                    arrive(n, kinds[n])
                    for t in range(4):
                        if t == 2 and kinds[n] == 2:
                            arrive(n, Y)
                        if t % 2 == 0:
                            block = ins[d, b, q, :, t // 2 * SIDE : (t // 2 + 1) * SIDE]
                        for m in range(2):
                            pltpu.matmul_acc_lhs(sums[2 * m + t % 2], block, t % 2)
                        if t < 2:
                            push(q, t + 2)
                        elif n + 1 < Y:
                            push(order[n + 1], t - 2)
                for h in range(2):
                    by_real, by_imag = pltpu.matmul_pop(sums[h]), pltpu.matmul_pop(sums[2 + h])
                    real = by_real[:width] - by_imag[width:]
                    imag = by_imag[:width] + by_real[width:]
                    cols = slice(h * SIDE, (h + 1) * SIDE)
                    fresh = jnp.concatenate([real, imag], 0) + src[slot, b, :, cols].astype(jnp.float32)
                    outs[d, b, :, cols] = fresh.astype(jnp.bfloat16)

            def compute():
                sums = [pltpu.ACC(mxu_id=n // 2)((2 * width, SIDE), jnp.float32) for n in range(4)]
                pl.run_scoped(run, *sums)

            @pl.when((pos > 0) & (pos < LAST))
            def _():
                compute()
                send_all()

            @pl.when(pos == LAST)
            def _():
                compute()

            if c == 1:

                @pl.when(slot == 2)
                def _():
                    for at in range(2):
                        swap_out(b, at).start()

            @pl.when(slot < 2)
            def _():
                half_copy(d, b, c).start()
                out_copy(d, b, c).start()

            return carry

        lax.fori_loop(begin, end, step, 0)
        drain(jnp.where(end == batches, first, second))

    def serve(c):
        def helps(d):
            return (worker_of(layer, d) != c) & (slot_of(d) < 2)

        def before():
            for d in (first, second):

                @pl.when(helps(d))
                def _():
                    src_copy(d, c).start()

            @pl.when(flipped)
            def _():
                swap_source(c).start()

        def offer(d):
            def then(p, q):
                @pl.when(helps(d))
                def _():
                    gt_copy(d, c, p, q).start()

                @pl.when(slot_of(d) == 2)
                def _():
                    swap_copy(c, p, q).start()

            transpose(d, c, then)

        def after():
            for d in (first, second):

                @pl.when(helps(d))
                def _():
                    def step(b, carry):
                        half_copy(d, b, 1 - c).wait_recv()
                        return carry

                    src_copy(d, c).wait_send()

                    @pl.when(position(d) > 0)
                    def _():
                        for_gt(lambda copy: copy.wait_send(), d, c)

                    lax.fori_loop(0, batches, step, 0)

            @pl.when(flipped)
            def _():
                def step(b, carry):
                    swap_out(b, c).wait_recv()
                    return carry

                swap_source(c).wait_send()
                for p in range(2):
                    for q in range(Y):
                        swap_copy(c, p, q).wait_send()
                lax.fori_loop(0, batches, step, 0)

        return before, offer, after

    for d in range(2):
        source_load(d).start()
    load(first)
    pl.semaphore_signal(barrier, 1, device_id=sibling, device_id_type=MESH)

    def skip(d):
        for p in range(2):
            load_wait(d, p)

    @pl.when(core == 0)
    def _():
        before, offer, after = serve(0)

        @pl.when(middle)
        def _():
            for hop in (-1, 1):
                greet(layer + hop, worker_of(layer + hop, 0))

        @pl.when(flipped)
        def _():
            pl.semaphore_signal(barrier, 1, device_id=(partner, 2 * y + 1), device_id_type=MESH)

        load(second)
        place_source(0)
        pl.semaphore_wait(barrier, 1 + jnp.where(middle, 2 * Y, 0) + jnp.where(flipped, 1, 0))
        before()

        @pl.when(position(first) > 0)
        def _():
            offer(first)

        @pl.when(position(first) == 0)
        def _():
            skip(first)

        offer(second)

        @pl.when(middle)
        def _():
            begin = jnp.where(first == 0, 0, batches)
            work(0, begin, begin + batches)

        after()

    @pl.when(core == 1)
    def _():
        before, offer, after = serve(1)
        guests = 0
        for hop in (-1, 1):
            inside = (layer + hop >= 0) & (layer + hop <= LAST)
            guests = guests + jnp.where(inside, Y, 0)

            @pl.when(inside)
            def _():
                greet(layer + hop, 1)

        near = (layer == MID - 2) | (layer == MID + 1)
        guests = guests + jnp.where(near, Y, 0)

        @pl.when(near)
        def _():
            greet(jnp.where(layer < MID, MID - 1, MID), 0)

        over = (layer == 3) | (layer == 4) | (layer == 11) | (layer == 12)
        under = (layer == 7) | (layer == 8) | (layer == 15) | (layer == 16)
        guests = guests + jnp.where(over | under, Y, 0) + jnp.where(flipped, 2, 0)

        @pl.when(over | under)
        def _():
            greet(jnp.where(over, layer + Y, layer - Y), 1)

        @pl.when(flipped)
        def _():
            for at in range(2):
                pl.semaphore_signal(barrier, 1, device_id=(partner, 2 * y + at), device_id_type=MESH)

        load(second)
        place_source(1)

        @pl.when((position(first) > 0) & jnp.logical_not(middle))
        def _():
            transpose(first, 1)

        @pl.when(position(first) == 0)
        def _():
            skip(first)

        pl.semaphore_wait(barrier, 1 + guests)
        before()

        @pl.when(middle)
        def _():
            offer(first)

        @pl.when(central)
        def _():
            offer(second)

        begin = jnp.where(middle & (first == 0), batches, 0)
        work(1, begin, jnp.where(middle & (first == 1), batches, 2 * batches))
        after()


def on_device(green_down, green_up, source_down, source_up):
    shots = source_down.shape[2]
    width = shots // BATCHES
    points = green_down.shape[3]
    any_space = pl.BlockSpec(memory_space=pl.ANY)
    dma = pltpu.SemaphoreType.DMA
    trace = (BATCHES, 2 * width, PIECE)
    out = pl.pallas_call(
        functools.partial(kernel, BATCHES),
        out_shape=jax.ShapeDtypeStruct((2, BATCHES, 2 * width, ROWS), jnp.bfloat16),
        in_specs=[any_space] * 4,
        out_specs=any_space,
        scratch_shapes=[
            pltpu.VMEM((2, 2, ROWS, points), jnp.bfloat16),
            pltpu.VMEM((2, 2, shots, ROWS), jnp.bfloat16),
            pltpu.VMEM((3, Y, PIECE, 2 * PIECE), jnp.bfloat16),
            pltpu.VMEM((3, *trace), jnp.bfloat16),
            pltpu.VMEM((2, BATCHES, Y, 2 * width, PIECE), jnp.bfloat16),
            pltpu.VMEM((2, *trace), jnp.bfloat16),
            dma((2, 2)),
            dma((2,)),
            dma((2, 2, Y)),
            dma((2, 2, Y)),
            dma((2,)),
            dma((2,)),
            dma((2, BATCHES, SENDS)),
            dma((2, BATCHES, SENDS)),
            dma((2, BATCHES)),
            dma((2, BATCHES)),
            dma((2, BATCHES)),
            dma((2, Y)),
            dma((2, 2, Y)),
            dma((3,)),
        ],
        compiler_params=pltpu.CompilerParams(
            collective_id=0, has_side_effects=True, vmem_limit_bytes=60 << 20
        ),
    )(green_down, green_up, source_down, source_up)
    out = out.reshape(2, BATCHES, 2, width, ROWS).transpose(0, 2, 1, 3, 4).reshape(2, 2, shots, ROWS)
    return out[0][None], out[1][None]


def solution(mesh):
    in_specs = (
        P("layer", None, "iface", None),
        P("layer", None, "iface", None),
        P("layer", None, None, "iface"),
        P("layer", None, None, "iface"),
    )
    out_specs = (P("layer", None, None, "iface"), P("layer", None, None, "iface"))
    return jax.shard_map(
        on_device, mesh=mesh, in_specs=in_specs, out_specs=out_specs, check_vma=False
    )
```

```python
import functools

import jax
import jax.numpy as jnp
from jax import lax
from jax.experimental import pallas as pl
from jax.experimental.pallas import tpu as pltpu
from jax.sharding import PartitionSpec as P

MESH = pl.DeviceIdType.MESH
LAYERS = 32
LAST = LAYERS - 1
MID = LAYERS // 2
Y = 4
ROWS = 256
PIECE = 2 * ROWS
SIDE = 256
BATCHES = 12
SENDS = Y + 1


def kernel(
    batches, gd_ref, gu_ref, sd_ref, su_ref, o_ref,
    graw, sraw, gt, src, ins, outs,
    g_sem, s_sem, gt_send, gt_recv, src_send, src_recv, send_sem, recv_sem, half_send, half_recv, o_sem,
    swap_send, swap_recv, swap_src,
):
    shots = sd_ref.shape[2]
    width = shots // batches
    layer = lax.axis_index("layer")
    iface = lax.axis_index("iface")
    y, core = iface // 2, lax.rem(iface, 2)
    sibling = (layer, 2 * y + 1 - core)
    first = jnp.where(layer < MID, 0, 1)
    second = 1 - first
    middle = (layer == MID - 1) | (layer == MID)
    central = (layer >= MID // 2) & (layer < LAYERS - MID // 2)

    def worker_of(at, d):
        return jnp.where(((at == MID - 1) | (at == MID)) & (d == 0), 0, 1)

    def flips(at, d):
        plane = at // Y
        return (d == 1) & ((plane == 1) | (plane == 3))

    def host(at, d):
        mirrored = at // Y * Y + Y - 1 - lax.rem(at, Y)
        return jnp.where(flips(at, d), mirrored, at)

    flipped = flips(layer, 1)
    partner = host(layer, 1)

    def position(d):
        return jnp.where(d == 0, layer, LAST - partner)

    def slot_of(d):
        return jnp.where(flipped & (d == 1), 2, d)

    def load(d):
        def start(ref, at):
            for p in range(2):
                pltpu.make_async_copy(ref.at[0, p], graw.at[at, p], g_sem.at[at, p]).start()

        @pl.when(d == 0)
        def _():
            start(gd_ref, 0)

        @pl.when(d == 1)
        def _():
            start(gu_ref, 1)

    def load_wait(d, p):
        pltpu.make_async_copy(gd_ref.at[0, p], graw.at[d, p], g_sem.at[d, p]).wait()

    def source_load(which, d):
        ref = (sd_ref, su_ref)[which]
        return pltpu.make_async_copy(ref.at[0], sraw.at[d], s_sem.at[d])

    def place_source(c, *sweeps):
        for d in sweeps:
            source_load(0, d).wait()
            for b in range(batches):
                rows = [sraw[d, p, b * width : (b + 1) * width, :].astype(jnp.float32) for p in range(2)]
                src[d, b, :, c * ROWS : (c + 1) * ROWS] = jnp.concatenate(rows, 0).astype(jnp.bfloat16)

    def transpose(d, c, then=None):
        for p in range(2):
            load_wait(d, p)

            def step(q, carry):
                block = graw[d, p, :, pl.ds(pl.multiple_of(q * PIECE, PIECE), PIECE)]
                gt[d, q, :, p * PIECE + c * ROWS : p * PIECE + (c + 1) * ROWS] = block.T
                if then is not None:
                    then(p, q)
                return carry

            lax.fori_loop(0, Y, step, 0)

    def remote(a, b, send, recv, to):
        return pltpu.make_async_remote_copy(a, b, send, recv, device_id=to, device_id_type=MESH)

    def gt_copy(d, c, p, q):
        half = gt.at[d, q, :, pl.ds(p * PIECE + c * ROWS, ROWS)]
        return remote(half, half, gt_send.at[d, p, q], gt_recv.at[d, p, q], sibling)

    def for_gt(act, d, c):
        for p in range(2):
            for q in range(Y):
                act(gt_copy(d, c, p, q))

    def src_copy(d, c):
        half = src.at[d, :, :, pl.ds(c * ROWS, ROWS)]
        return remote(half, half, src_send.at[d], src_recv.at[d], sibling)

    def swap_copy(c, p, q):
        cols = pl.ds(p * PIECE + c * ROWS, ROWS)
        a, z = gt.at[1, q, :, cols], gt.at[2, q, :, cols]
        return remote(a, z, swap_send.at[p, q], swap_recv.at[c, p, q], (partner, 2 * y + 1))

    def swap_source(c):
        cols = pl.ds(c * ROWS, ROWS)
        a, z = src.at[1, :, :, cols], src.at[2, :, :, cols]
        return remote(a, z, swap_src.at[2], swap_src.at[c], (partner, 2 * y + 1))

    def pair(j):
        return pl.ds(2 * j, 2)

    def swap_out(j, c):
        half = outs.at[1, pair(j), :, pl.ds(c * ROWS, ROWS)]
        sem = (half_send, o_sem)[c].at[1, j]
        return remote(half, o_ref.at[1, pair(j)], sem, half_recv.at[1, j], (partner, 2 * y + c))

    def half_copy(d, j, c):
        half = outs.at[d, pair(j), :, pl.ds((1 - c) * ROWS, ROWS)]
        return remote(half, o_ref.at[d, pair(j)], half_send.at[d, j], half_recv.at[d, j], sibling)

    def out_copy(d, j, c):
        half = outs.at[d, pair(j), :, pl.ds(c * ROWS, ROWS)]
        return pltpu.make_async_copy(half, o_ref.at[d, pair(j)], o_sem.at[d, j])

    barrier = pltpu.get_barrier_semaphore()

    def greet(at, c):
        for q in range(Y):
            pl.semaphore_signal(barrier, 1, device_id=(at, 2 * q + c), device_id_type=MESH)

    def targets(d):
        at = jnp.where(d == 0, layer + 1, host(jnp.maximum(partner - 1, 0), 1))
        worker = worker_of(at, d)
        return [(at, 2 * lax.rem(y + off, Y) + worker) for off in range(Y)]

    def send(d, b, kind, to):
        off = 2 if kind == Y else kind
        a, z = outs.at[d, b], ins.at[d, b, y]
        if off == 2:
            cols = pl.ds(SIDE if kind == Y else 0, SIDE)
            a, z = outs.at[d, b, :, cols], ins.at[d, b, y, :, cols]
        return remote(a, z, send_sem.at[d, b, kind], recv_sem.at[d, b, kind], to[off])

    def work(c, begin, end):
        def mine(d):
            return worker_of(layer, d) == c

        @pl.when(mine(first))
        def _():
            src_copy(first, 1 - c).wait_recv()

        @pl.when(mine(first) & (position(first) > 0))
        def _():
            for_gt(lambda copy: copy.wait_recv(), first, 1 - c)

        def drain(d):
            def step(b, carry):
                @pl.when(position(d) < LAST)
                def _():
                    for kind in range(SENDS):
                        send(d, b, kind, targets(d)).wait_send()

                return carry

            def written(j, carry):
                if c == 1:

                    @pl.when(slot_of(d) == 2)
                    def _():
                        for at in range(2):
                            swap_out(j, at).wait_send()

                @pl.when(slot_of(d) < 2)
                def _():
                    half_copy(d, j, c).wait_send()
                    out_copy(d, j, c).wait()

                return carry

            lax.fori_loop(0, batches, step, 0)
            lax.fori_loop(0, batches // 2, written, 0)

        def step(k, carry):
            d = jnp.where(k < batches, first, second)
            b = lax.rem(k, batches)
            pos = position(d)
            slot = slot_of(d)
            to = targets(d)

            def send_all():
                for kind in (2, Y, 1, 3, 0):
                    send(d, b, kind, to).start()

            @pl.when(k == batches)
            def _():
                if c == 1:

                    @pl.when(jnp.logical_not(central))
                    def _():
                        def then(p, q):
                            @pl.when(flipped)
                            def _():
                                swap_copy(c, p, q).start()

                        transpose(second, c, then)

                    @pl.when(begin == 0)
                    def _():
                        drain(first)

                if c == 1:

                    @pl.when(flipped)
                    def _():
                        for at in range(2):
                            swap_source(at).wait_recv()
                            for p in range(2):
                                for q in range(Y):
                                    swap_copy(at, p, q).wait_recv()

                @pl.when(slot_of(second) < 2)
                def _():
                    src_copy(second, 1 - c).wait_recv()
                    for_gt(lambda copy: copy.wait_recv(), second, 1 - c)

            @pl.when(pos == 0)
            def _():
                outs[d, b] = src[d, b]
                send_all()

            def run(*sums):
                order = [lax.rem(y + off, Y) for off in (0, 1, 3, 2)]
                kinds = (0, 3, 1, 2)

                def push(q, t):
                    rows = slice(t // 2 * SIDE, (t // 2 + 1) * SIDE)
                    for m in range(2):
                        at = (2 * m + t % 2) * SIDE
                        pltpu.matmul_push_rhs(gt[slot, q, rows, at : at + SIDE], t % 2, m)

                def arrive(n, kind):
                    part = (d, b, order[n])
                    ref = ins.at[part]
                    if kind in (2, Y):
                        ref = ins.at[(*part, slice(None), pl.ds(SIDE if kind == Y else 0, SIDE))]
                    remote(ref, ref, send_sem.at[d, b, kind], recv_sem.at[d, b, kind], sibling).wait_recv()

                push(order[0], 0)
                push(order[0], 1)
                for n, q in enumerate(order):
                    arrive(n, kinds[n])
                    for t in range(4):
                        if t == 2 and kinds[n] == 2:
                            arrive(n, Y)
                        if t % 2 == 0:
                            block = ins[d, b, q, :, t // 2 * SIDE : (t // 2 + 1) * SIDE]
                        for m in range(2):
                            pltpu.matmul_acc_lhs(sums[2 * m + t % 2], block, t % 2)
                        if t < 2:
                            push(q, t + 2)
                        elif n + 1 < Y:
                            push(order[n + 1], t - 2)
                for h in range(2):
                    by_real, by_imag = pltpu.matmul_pop(sums[h]), pltpu.matmul_pop(sums[2 + h])
                    real = by_real[:width] - by_imag[width:]
                    imag = by_imag[:width] + by_real[width:]
                    cols = slice(h * SIDE, (h + 1) * SIDE)
                    fresh = jnp.concatenate([real, imag], 0) + src[slot, b, :, cols].astype(jnp.float32)
                    outs[d, b, :, cols] = fresh.astype(jnp.bfloat16)

            def compute():
                sums = [pltpu.ACC(mxu_id=n // 2)((2 * width, SIDE), jnp.float32) for n in range(4)]
                pl.run_scoped(run, *sums)

            @pl.when((pos > 0) & (pos < LAST))
            def _():
                compute()
                send_all()

            @pl.when(pos == LAST)
            def _():
                compute()

            both, j = lax.rem(b, 2) == 1, b // 2
            if c == 1:

                @pl.when(both & (slot == 2))
                def _():
                    for at in range(2):
                        swap_out(j, at).start()

            @pl.when(both & (slot < 2))
            def _():
                half_copy(d, j, c).start()
                out_copy(d, j, c).start()

            return carry

        lax.fori_loop(begin, end, step, 0)
        drain(jnp.where(end == batches, first, second))

    def serve(c):
        def helps(d):
            return (worker_of(layer, d) != c) & (slot_of(d) < 2)

        def before():
            @pl.when(helps(first))
            def _():
                src_copy(first, c).start()

            place_source(c, second)

            @pl.when(helps(second))
            def _():
                src_copy(second, c).start()

            @pl.when(flipped)
            def _():
                swap_source(c).start()

        def offer(d):
            def then(p, q):
                @pl.when(helps(d))
                def _():
                    gt_copy(d, c, p, q).start()

                @pl.when(slot_of(d) == 2)
                def _():
                    swap_copy(c, p, q).start()

            transpose(d, c, then)

        def after():
            for d in (first, second):

                @pl.when(helps(d))
                def _():
                    def step(j, carry):
                        half_copy(d, j, 1 - c).wait_recv()
                        return carry

                    src_copy(d, c).wait_send()

                    @pl.when(position(d) > 0)
                    def _():
                        for_gt(lambda copy: copy.wait_send(), d, c)

                    lax.fori_loop(0, batches // 2, step, 0)

            @pl.when(flipped)
            def _():
                def step(j, carry):
                    swap_out(j, c).wait_recv()
                    return carry

                swap_source(c).wait_send()
                for p in range(2):
                    for q in range(Y):
                        swap_copy(c, p, q).wait_send()
                lax.fori_loop(0, batches // 2, step, 0)

        return before, offer, after

    for d in range(2):
        source_load(d, d).start()
    load(first)
    pl.semaphore_signal(barrier, 1, device_id=sibling, device_id_type=MESH)

    def skip(d):
        for p in range(2):
            load_wait(d, p)

    @pl.when(core == 0)
    def _():
        before, offer, after = serve(0)

        @pl.when(middle)
        def _():
            for hop in (-1, 1):
                greet(layer + hop, worker_of(layer + hop, 0))

        @pl.when(flipped)
        def _():
            pl.semaphore_signal(barrier, 1, device_id=(partner, 2 * y + 1), device_id_type=MESH)

        load(second)
        place_source(0, first)
        pl.semaphore_wait(barrier, 1 + jnp.where(middle, 2 * Y, 0) + jnp.where(flipped, 1, 0))
        before()

        @pl.when(position(first) > 0)
        def _():
            offer(first)

        @pl.when(position(first) == 0)
        def _():
            skip(first)

        offer(second)

        @pl.when(middle)
        def _():
            begin = jnp.where(first == 0, 0, batches)
            work(0, begin, begin + batches)

        after()

    @pl.when(core == 1)
    def _():
        before, offer, after = serve(1)
        guests = 0
        for hop in (-1, 1):
            inside = (layer + hop >= 0) & (layer + hop <= LAST)
            guests = guests + jnp.where(inside, Y, 0)

            @pl.when(inside)
            def _():
                greet(layer + hop, 1)

        near = (layer == MID - 2) | (layer == MID + 1)
        guests = guests + jnp.where(near, Y, 0)

        @pl.when(near)
        def _():
            greet(jnp.where(layer < MID, MID - 1, MID), 0)

        over = (layer == 3) | (layer == 4) | (layer == 11) | (layer == 12)
        under = (layer == 7) | (layer == 8) | (layer == 15) | (layer == 16)
        guests = guests + jnp.where(over | under, Y, 0) + jnp.where(flipped, 2, 0)

        @pl.when(over | under)
        def _():
            greet(jnp.where(over, layer + Y, layer - Y), 1)

        @pl.when(flipped)
        def _():
            for at in range(2):
                pl.semaphore_signal(barrier, 1, device_id=(partner, 2 * y + at), device_id_type=MESH)

        load(second)
        place_source(1, first)

        @pl.when((position(first) > 0) & jnp.logical_not(middle))
        def _():
            transpose(first, 1)

        @pl.when(position(first) == 0)
        def _():
            skip(first)

        pl.semaphore_wait(barrier, 1 + guests)
        before()

        @pl.when(middle)
        def _():
            offer(first)

        @pl.when(central)
        def _():
            offer(second)

        begin = jnp.where(middle & (first == 0), batches, 0)
        work(1, begin, jnp.where(middle & (first == 1), batches, 2 * batches))
        after()


def on_device(green_down, green_up, source_down, source_up):
    shots = source_down.shape[2]
    width = shots // BATCHES
    points = green_down.shape[3]
    any_space = pl.BlockSpec(memory_space=pl.ANY)
    dma = pltpu.SemaphoreType.DMA
    trace = (BATCHES, 2 * width, PIECE)
    out = pl.pallas_call(
        functools.partial(kernel, BATCHES),
        out_shape=jax.ShapeDtypeStruct((2, BATCHES, 2 * width, ROWS), jnp.bfloat16),
        in_specs=[any_space] * 4,
        out_specs=any_space,
        scratch_shapes=[
            pltpu.VMEM((2, 2, ROWS, points), jnp.bfloat16),
            pltpu.VMEM((2, 2, shots, ROWS), jnp.bfloat16),
            pltpu.VMEM((3, Y, PIECE, 2 * PIECE), jnp.bfloat16),
            pltpu.VMEM((3, *trace), jnp.bfloat16),
            pltpu.VMEM((2, BATCHES, Y, 2 * width, PIECE), jnp.bfloat16),
            pltpu.VMEM((2, *trace), jnp.bfloat16),
            dma((2, 2)),
            dma((2,)),
            dma((2, 2, Y)),
            dma((2, 2, Y)),
            dma((2,)),
            dma((2,)),
            dma((2, BATCHES, SENDS)),
            dma((2, BATCHES, SENDS)),
            dma((2, BATCHES // 2)),
            dma((2, BATCHES // 2)),
            dma((2, BATCHES // 2)),
            dma((2, Y)),
            dma((2, 2, Y)),
            dma((3,)),
        ],
        compiler_params=pltpu.CompilerParams(
            collective_id=0, has_side_effects=True, vmem_limit_bytes=60 << 20
        ),
    )(green_down, green_up, source_down, source_up)
    out = out.reshape(2, BATCHES, 2, width, ROWS).transpose(0, 2, 1, 3, 4).reshape(2, 2, shots, ROWS)
    return out[0][None], out[1][None]


def solution(mesh):
    in_specs = (
        P("layer", None, "iface", None),
        P("layer", None, "iface", None),
        P("layer", None, None, "iface"),
        P("layer", None, None, "iface"),
    )
    out_specs = (P("layer", None, None, "iface"), P("layer", None, None, "iface"))
    return jax.shard_map(
        on_device, mesh=mesh, in_specs=in_specs, out_specs=out_specs, check_vma=False
    )
```

```python
import functools

import jax
import jax.numpy as jnp
from jax import lax
from jax.experimental import pallas as pl
from jax.experimental.pallas import tpu as pltpu
from jax.sharding import PartitionSpec as P

MESH = pl.DeviceIdType.MESH
LAYERS = 32
LAST = LAYERS - 1
MID = LAYERS // 2
Y = 4
ROWS = 256
PIECE = 2 * ROWS
SIDE = 256
BATCHES = 12
SENDS = Y + 1


def kernel(
    batches, gd_ref, gu_ref, sd_ref, su_ref, o_ref,
    graw, sraw, gt, src, ins, outs,
    g_sem, s_sem, gt_send, gt_recv, src_send, src_recv, send_sem, recv_sem, half_send, half_recv, o_sem,
    swap_send, swap_recv, swap_src,
):
    shots = sd_ref.shape[2]
    width = shots // batches
    layer = lax.axis_index("layer")
    iface = lax.axis_index("iface")
    y, core = iface // 2, lax.rem(iface, 2)
    sibling = (layer, 2 * y + 1 - core)
    first = jnp.where(layer < MID, 0, 1)
    second = 1 - first
    middle = (layer == MID - 1) | (layer == MID)
    central = (layer >= MID // 2) & (layer < LAYERS - MID // 2)

    def worker_of(at, d):
        return jnp.where(((at == MID - 1) | (at == MID)) & (d == 0), 0, 1)

    def flips(at, d):
        plane = at // Y
        return (d == 1) & ((plane == 1) | (plane == 3))

    def host(at, d):
        mirrored = at // Y * Y + Y - 1 - lax.rem(at, Y)
        return jnp.where(flips(at, d), mirrored, at)

    flipped = flips(layer, 1)
    partner = host(layer, 1)

    def position(d):
        return jnp.where(d == 0, layer, LAST - partner)

    def slot_of(d):
        return jnp.where(flipped & (d == 1), 2, d)

    def load(d):
        def start(ref, at):
            for p in range(2):
                pltpu.make_async_copy(ref.at[0, p], graw.at[at, p], g_sem.at[at, p]).start()

        @pl.when(d == 0)
        def _():
            start(gd_ref, 0)

        @pl.when(d == 1)
        def _():
            start(gu_ref, 1)

    def load_wait(d, p):
        pltpu.make_async_copy(gd_ref.at[0, p], graw.at[d, p], g_sem.at[d, p]).wait()

    def source_load(which, d):
        ref = (sd_ref, su_ref)[which]
        return pltpu.make_async_copy(ref.at[0], sraw.at[d], s_sem.at[d])

    def place_source(c, *sweeps):
        for d in sweeps:
            source_load(0, d).wait()
            for j in range(batches // 2):
                both = [sraw[d, p, 2 * j * width : 2 * (j + 1) * width, :].astype(jnp.float32) for p in range(2)]
                for h in range(2):
                    rows = [part[h * width : (h + 1) * width] for part in both]
                    placed = jnp.concatenate(rows, 0).astype(jnp.bfloat16)
                    src[d, 2 * j + h, :, c * ROWS : (c + 1) * ROWS] = placed

    def transpose(d, c, then=None):
        for p in range(2):
            load_wait(d, p)

            def step(q, carry):
                block = graw[d, p, :, pl.ds(pl.multiple_of(q * PIECE, PIECE), PIECE)]
                gt[d, q, :, p * PIECE + c * ROWS : p * PIECE + (c + 1) * ROWS] = block.T
                if then is not None:
                    then(p, q)
                return carry

            lax.fori_loop(0, Y, step, 0)

    def remote(a, b, send, recv, to):
        return pltpu.make_async_remote_copy(a, b, send, recv, device_id=to, device_id_type=MESH)

    def gt_copy(d, c, p, q):
        half = gt.at[d, q, :, pl.ds(p * PIECE + c * ROWS, ROWS)]
        return remote(half, half, gt_send.at[d, p, q], gt_recv.at[d, p, q], sibling)

    def for_gt(act, d, c):
        for p in range(2):
            for q in range(Y):
                act(gt_copy(d, c, p, q))

    def src_copy(d, c):
        half = src.at[d, :, :, pl.ds(c * ROWS, ROWS)]
        return remote(half, half, src_send.at[d], src_recv.at[d], sibling)

    def swap_copy(c, p, q):
        cols = pl.ds(p * PIECE + c * ROWS, ROWS)
        a, z = gt.at[1, q, :, cols], gt.at[2, q, :, cols]
        return remote(a, z, swap_send.at[p, q], swap_recv.at[c, p, q], (partner, 2 * y + 1))

    def swap_source(c):
        cols = pl.ds(c * ROWS, ROWS)
        a, z = src.at[1, :, :, cols], src.at[2, :, :, cols]
        return remote(a, z, swap_src.at[2], swap_src.at[c], (partner, 2 * y + 1))

    def pair(j):
        return pl.ds(2 * j, 2)

    def swap_out(j, c):
        half = outs.at[1, pair(j), :, pl.ds(c * ROWS, ROWS)]
        sem = (half_send, o_sem)[c].at[1, j]
        return remote(half, o_ref.at[1, pair(j)], sem, half_recv.at[1, j], (partner, 2 * y + c))

    def half_copy(d, j, c):
        half = outs.at[d, pair(j), :, pl.ds((1 - c) * ROWS, ROWS)]
        return remote(half, o_ref.at[d, pair(j)], half_send.at[d, j], half_recv.at[d, j], sibling)

    def out_copy(d, j, c):
        half = outs.at[d, pair(j), :, pl.ds(c * ROWS, ROWS)]
        return pltpu.make_async_copy(half, o_ref.at[d, pair(j)], o_sem.at[d, j])

    barrier = pltpu.get_barrier_semaphore()

    def greet(at, c):
        for q in range(Y):
            pl.semaphore_signal(barrier, 1, device_id=(at, 2 * q + c), device_id_type=MESH)

    def targets(d):
        at = jnp.where(d == 0, layer + 1, host(jnp.maximum(partner - 1, 0), 1))
        worker = worker_of(at, d)
        return [(at, 2 * lax.rem(y + off, Y) + worker) for off in range(Y)]

    def send(d, b, kind, to):
        off = 2 if kind == Y else kind
        a, z = outs.at[d, b], ins.at[d, b, y]
        if off == 2:
            cols = pl.ds(SIDE if kind == Y else 0, SIDE)
            a, z = outs.at[d, b, :, cols], ins.at[d, b, y, :, cols]
        return remote(a, z, send_sem.at[d, b, kind], recv_sem.at[d, b, kind], to[off])

    def work(c, begin, end):
        def mine(d):
            return worker_of(layer, d) == c

        @pl.when(mine(first))
        def _():
            src_copy(first, 1 - c).wait_recv()

        @pl.when(mine(first) & (position(first) > 0))
        def _():
            for_gt(lambda copy: copy.wait_recv(), first, 1 - c)

        def drain(d):
            def step(b, carry):
                @pl.when(position(d) < LAST)
                def _():
                    for kind in range(SENDS):
                        send(d, b, kind, targets(d)).wait_send()

                return carry

            def written(j, carry):
                if c == 1:

                    @pl.when(slot_of(d) == 2)
                    def _():
                        for at in range(2):
                            swap_out(j, at).wait_send()

                @pl.when(slot_of(d) < 2)
                def _():
                    half_copy(d, j, c).wait_send()
                    out_copy(d, j, c).wait()

                return carry

            lax.fori_loop(0, batches, step, 0)
            lax.fori_loop(0, batches // 2, written, 0)

        def step(k, carry):
            d = jnp.where(k < batches, first, second)
            b = lax.rem(k, batches)
            pos = position(d)
            slot = slot_of(d)
            to = targets(d)

            def send_all():
                for kind in (2, Y, 1, 3, 0):
                    send(d, b, kind, to).start()

            @pl.when(k == batches)
            def _():
                if c == 1:

                    @pl.when(jnp.logical_not(central))
                    def _():
                        def then(p, q):
                            @pl.when(flipped)
                            def _():
                                swap_copy(c, p, q).start()

                        transpose(second, c, then)

                    @pl.when(begin == 0)
                    def _():
                        drain(first)

                if c == 1:

                    @pl.when(flipped)
                    def _():
                        for at in range(2):
                            swap_source(at).wait_recv()
                            for p in range(2):
                                for q in range(Y):
                                    swap_copy(at, p, q).wait_recv()

                @pl.when(slot_of(second) < 2)
                def _():
                    src_copy(second, 1 - c).wait_recv()
                    for_gt(lambda copy: copy.wait_recv(), second, 1 - c)

            @pl.when(pos == 0)
            def _():
                outs[d, b] = src[d, b]
                send_all()

            def run(*sums):
                order = [lax.rem(y + off, Y) for off in (0, 1, 3, 2)]
                kinds = (0, 3, 1, 2)

                def push(q, t):
                    rows = slice(t // 2 * SIDE, (t // 2 + 1) * SIDE)
                    for m in range(2):
                        at = (2 * m + t % 2) * SIDE
                        pltpu.matmul_push_rhs(gt[slot, q, rows, at : at + SIDE], t % 2, m)

                def arrive(n, kind):
                    part = (d, b, order[n])
                    ref = ins.at[part]
                    if kind in (2, Y):
                        ref = ins.at[(*part, slice(None), pl.ds(SIDE if kind == Y else 0, SIDE))]
                    remote(ref, ref, send_sem.at[d, b, kind], recv_sem.at[d, b, kind], sibling).wait_recv()

                push(order[0], 0)
                push(order[0], 1)
                for n, q in enumerate(order):
                    arrive(n, kinds[n])
                    for t in range(4):
                        if t == 2 and kinds[n] == 2:
                            arrive(n, Y)
                        if t % 2 == 0:
                            block = ins[d, b, q, :, t // 2 * SIDE : (t // 2 + 1) * SIDE]
                        for m in range(2):
                            pltpu.matmul_acc_lhs(sums[2 * m + t % 2], block, t % 2)
                        if t < 2:
                            push(q, t + 2)
                        elif n + 1 < Y:
                            push(order[n + 1], t - 2)
                for h in range(2):
                    by_real, by_imag = pltpu.matmul_pop(sums[h]), pltpu.matmul_pop(sums[2 + h])
                    real = by_real[:width] - by_imag[width:]
                    imag = by_imag[:width] + by_real[width:]
                    cols = slice(h * SIDE, (h + 1) * SIDE)
                    fresh = jnp.concatenate([real, imag], 0) + src[slot, b, :, cols].astype(jnp.float32)
                    outs[d, b, :, cols] = fresh.astype(jnp.bfloat16)

            def compute():
                sums = [pltpu.ACC(mxu_id=n // 2)((2 * width, SIDE), jnp.float32) for n in range(4)]
                pl.run_scoped(run, *sums)

            @pl.when((pos > 0) & (pos < LAST))
            def _():
                compute()
                send_all()

            @pl.when(pos == LAST)
            def _():
                compute()

            both, j = lax.rem(b, 2) == 1, b // 2
            if c == 1:

                @pl.when(both & (slot == 2))
                def _():
                    for at in range(2):
                        swap_out(j, at).start()

            @pl.when(both & (slot < 2))
            def _():
                half_copy(d, j, c).start()
                out_copy(d, j, c).start()

            return carry

        lax.fori_loop(begin, end, step, 0)
        drain(jnp.where(end == batches, first, second))

    def serve(c):
        def helps(d):
            return (worker_of(layer, d) != c) & (slot_of(d) < 2)

        def before():
            @pl.when(helps(first))
            def _():
                src_copy(first, c).start()

            place_source(c, second)

            @pl.when(helps(second))
            def _():
                src_copy(second, c).start()

            @pl.when(flipped)
            def _():
                swap_source(c).start()

        def offer(d):
            def then(p, q):
                @pl.when(helps(d))
                def _():
                    gt_copy(d, c, p, q).start()

                @pl.when(slot_of(d) == 2)
                def _():
                    swap_copy(c, p, q).start()

            transpose(d, c, then)

        def after():
            for d in (first, second):

                @pl.when(helps(d))
                def _():
                    def step(j, carry):
                        half_copy(d, j, 1 - c).wait_recv()
                        return carry

                    src_copy(d, c).wait_send()

                    @pl.when(position(d) > 0)
                    def _():
                        for_gt(lambda copy: copy.wait_send(), d, c)

                    lax.fori_loop(0, batches // 2, step, 0)

            @pl.when(flipped)
            def _():
                def step(j, carry):
                    swap_out(j, c).wait_recv()
                    return carry

                swap_source(c).wait_send()
                for p in range(2):
                    for q in range(Y):
                        swap_copy(c, p, q).wait_send()
                lax.fori_loop(0, batches // 2, step, 0)

        return before, offer, after

    for d in range(2):
        source_load(d, d).start()
    load(first)
    pl.semaphore_signal(barrier, 1, device_id=sibling, device_id_type=MESH)

    def skip(d):
        for p in range(2):
            load_wait(d, p)

    @pl.when(core == 0)
    def _():
        before, offer, after = serve(0)

        @pl.when(middle)
        def _():
            for hop in (-1, 1):
                greet(layer + hop, worker_of(layer + hop, 0))

        @pl.when(flipped)
        def _():
            pl.semaphore_signal(barrier, 1, device_id=(partner, 2 * y + 1), device_id_type=MESH)

        load(second)
        place_source(0, first)
        pl.semaphore_wait(barrier, 1 + jnp.where(middle, 2 * Y, 0) + jnp.where(flipped, 1, 0))
        before()

        @pl.when(position(first) > 0)
        def _():
            offer(first)

        @pl.when(position(first) == 0)
        def _():
            skip(first)

        offer(second)

        @pl.when(middle)
        def _():
            begin = jnp.where(first == 0, 0, batches)
            work(0, begin, begin + batches)

        after()

    @pl.when(core == 1)
    def _():
        before, offer, after = serve(1)
        guests = 0
        for hop in (-1, 1):
            inside = (layer + hop >= 0) & (layer + hop <= LAST)
            guests = guests + jnp.where(inside, Y, 0)

            @pl.when(inside)
            def _():
                greet(layer + hop, 1)

        near = (layer == MID - 2) | (layer == MID + 1)
        guests = guests + jnp.where(near, Y, 0)

        @pl.when(near)
        def _():
            greet(jnp.where(layer < MID, MID - 1, MID), 0)

        over = (layer == 3) | (layer == 4) | (layer == 11) | (layer == 12)
        under = (layer == 7) | (layer == 8) | (layer == 15) | (layer == 16)
        guests = guests + jnp.where(over | under, Y, 0) + jnp.where(flipped, 2, 0)

        @pl.when(over | under)
        def _():
            greet(jnp.where(over, layer + Y, layer - Y), 1)

        @pl.when(flipped)
        def _():
            for at in range(2):
                pl.semaphore_signal(barrier, 1, device_id=(partner, 2 * y + at), device_id_type=MESH)

        load(second)
        place_source(1, first)

        @pl.when((position(first) > 0) & jnp.logical_not(middle))
        def _():
            transpose(first, 1)

        @pl.when(position(first) == 0)
        def _():
            skip(first)

        pl.semaphore_wait(barrier, 1 + guests)
        before()

        @pl.when(middle)
        def _():
            offer(first)

        @pl.when(central)
        def _():
            offer(second)

        begin = jnp.where(middle & (first == 0), batches, 0)
        work(1, begin, jnp.where(middle & (first == 1), batches, 2 * batches))
        after()


def on_device(green_down, green_up, source_down, source_up):
    shots = source_down.shape[2]
    width = shots // BATCHES
    points = green_down.shape[3]
    any_space = pl.BlockSpec(memory_space=pl.ANY)
    dma = pltpu.SemaphoreType.DMA
    trace = (BATCHES, 2 * width, PIECE)
    out = pl.pallas_call(
        functools.partial(kernel, BATCHES),
        out_shape=jax.ShapeDtypeStruct((2, BATCHES, 2 * width, ROWS), jnp.bfloat16),
        in_specs=[any_space] * 4,
        out_specs=any_space,
        scratch_shapes=[
            pltpu.VMEM((2, 2, ROWS, points), jnp.bfloat16),
            pltpu.VMEM((2, 2, shots, ROWS), jnp.bfloat16),
            pltpu.VMEM((3, Y, PIECE, 2 * PIECE), jnp.bfloat16),
            pltpu.VMEM((3, *trace), jnp.bfloat16),
            pltpu.VMEM((2, BATCHES, Y, 2 * width, PIECE), jnp.bfloat16),
            pltpu.VMEM((2, *trace), jnp.bfloat16),
            dma((2, 2)),
            dma((2,)),
            dma((2, 2, Y)),
            dma((2, 2, Y)),
            dma((2,)),
            dma((2,)),
            dma((2, BATCHES, SENDS)),
            dma((2, BATCHES, SENDS)),
            dma((2, BATCHES // 2)),
            dma((2, BATCHES // 2)),
            dma((2, BATCHES // 2)),
            dma((2, Y)),
            dma((2, 2, Y)),
            dma((3,)),
        ],
        compiler_params=pltpu.CompilerParams(
            collective_id=0, has_side_effects=True, vmem_limit_bytes=60 << 20
        ),
    )(green_down, green_up, source_down, source_up)
    out = out.reshape(2, BATCHES, 2, width, ROWS).transpose(0, 2, 1, 3, 4).reshape(2, 2, shots, ROWS)
    return out[0][None], out[1][None]


def solution(mesh):
    in_specs = (
        P("layer", None, "iface", None),
        P("layer", None, "iface", None),
        P("layer", None, None, "iface"),
        P("layer", None, None, "iface"),
    )
    out_specs = (P("layer", None, None, "iface"), P("layer", None, None, "iface"))
    return jax.shard_map(
        on_device, mesh=mesh, in_specs=in_specs, out_specs=out_specs, check_vma=False
    )
```
